32 devices in a mesh: groups: 2 (over y), wide: 8 (over z, x), narrow: 2 (over core).
Axes of the slice: x: 2, y: 2, z: 4, core: 2. Of those that a mesh axis runs over, the one named last changes fastest.
Arguments:
- pieces: bfloat16 [2, 1024, 8192], P(None, ('groups', 'wide'), 'narrow'), parts along dimension 1, may hold values from -6 to 6
- destination: int32 [512], P('wide'), may hold values from 0 to 511, as said below
- first_offset: int32 [512], P('wide'), may hold values from 0 to 6144, as said below
- valid_length: int32 [512], P('wide'), may hold values from 2048 to 8192
- midpoint_factor: float32 [1024, 128], P(('groups', 'wide')), parts along dimension 0, may hold values from -0.3 to 0.3
- offset_factor: float32 [16384, 128], P(('groups', 'narrow')), parts along dimension 0, may hold values from -6 to 6
- threshold: float32 [16384], P(('groups', 'narrow')), parts along dimension 0, may hold values from 0.3 to 3
Outputs:
- sparse: bfloat16 [2, 1024, 8192], P(None, ('groups', 'wide'), 'narrow'), parts along dimension 1
- new_midpoint: float32 [1024, 128], P(('groups', 'wide')), parts along dimension 0
- new_offset: float32 [16384, 128], P(('groups', 'narrow')), parts along dimension 0
The draws below stay inside these ranges and needn't reach their ends.
There are 2 independent parts, one for each index of `groups`. The reference program is written for one: setup_inputs(seed, part) draws one part's arguments, and reference() takes and returns one part's arrays. A program takes and returns all parts, laid end to end along the dimension named above; an argument that names none is the same for every part. Nothing has to cross between parts.
Inputs may be any that keep to these rules, and one draw needn't show every extreme that they name: destination is a permutation of the midpoint rows; the 64 segments of one device (aligned blocks) name at most 16 rows of any aligned block of 64 midpoint rows, and exactly 16 rows of some block. first_offset + valid_length <= 8192.
All inputs are finite; a program needn't handle non-finite values.
Results may differ from the reference program's by a relative error of at most 0.005.
Values may be sent and summed in bfloat16 or wider, within the bound.
A program may use at most 64 MiB of HBM per device.

```python
import math
from functools import partial
import jax
import jax.numpy as jnp
from jax import lax

OFF = 8192
RANK = 64
ROWS_DEV = 64
ITERS = 2
MIDS = 512


def shuffled(count, subkey):
    return jax.random.permutation(subkey, count).astype(jnp.int32)


def route_table(key):
    block_count = MIDS // ROWS_DEV
    average = ROWS_DEV // block_count
    keys = jax.random.split(jax.random.fold_in(key, 11), 3)
    order = jax.random.permutation(keys[0], block_count).astype(jnp.int32)
    follow = jnp.roll(order, -1)
    column = jnp.arange(block_count, dtype=jnp.int32)
    counts = average + average * (column[None, :] == order[:, None]).astype(jnp.int32) - average * (column[None, :] == follow[:, None]).astype(jnp.int32)
    cumulative = jnp.cumsum(counts, axis=1)
    src_begin = cumulative - counts
    dst_begin = jnp.cumsum(counts, axis=0) - counts
    position = jnp.arange(ROWS_DEV, dtype=jnp.int32)
    target = jnp.sum((cumulative[:, None, :] <= position[None, :, None]).astype(jnp.int32), axis=2)
    within = position[None, :] - jnp.take_along_axis(src_begin, target, 1)
    arrival = jnp.take_along_axis(dst_begin, target, 1) + within
    local_orders = jax.vmap(partial(shuffled, ROWS_DEV))(jax.random.split(keys[1], block_count))
    landing = local_orders[target, arrival]
    value = target * ROWS_DEV + landing
    senders = jax.vmap(partial(shuffled, ROWS_DEV))(jax.random.split(keys[2], block_count))
    table = jnp.zeros((block_count, ROWS_DEV), jnp.int32)
    table = table.at[column[:, None], senders].set(value)
    return table.reshape(MIDS)


def segment_table(key):
    keys = jax.random.split(jax.random.fold_in(key, 23), 2)
    valid = jax.random.randint(keys[0], (MIDS,), OFF // 4, OFF + 1, dtype=jnp.int32)
    begin = jax.random.randint(keys[1], (MIDS,), 0, OFF + 1, dtype=jnp.int32) % (OFF - valid + 1)
    return (begin, valid)


def draw_destination(key, part):
    return route_table(key)


def draw_first_offset(key, part):
    return segment_table(key)[0]


def draw_valid_length(key, part):
    return segment_table(key)[1]


def block_levels(key, shape, shards, least, largest):
    def one(dim, parts):
        steps = jax.random.uniform(jax.random.fold_in(jax.random.fold_in(key, 6), dim), (parts,), jnp.float32, least / len(shards), largest / len(shards))
        return jnp.repeat(jnp.exp(steps), shape[dim] // parts).reshape((-1,) + (1,) * (len(shape) - dim - 1))

    level = one(*shards[0])
    for cut in shards[1:]:
        level = level * one(*cut)
    return level


def bell_draw(own_key, dims, spread, limit, shards=(), kind=jnp.bfloat16):
    loudness = block_levels(own_key, dims, shards, -0.22, 0.18) if shards else 1.0
    array = jax.random.normal(own_key, dims, jnp.float32) * spread * loudness
    return jnp.minimum(jnp.maximum(array, -limit), limit).astype(kind)


def setup_inputs(seed: int = 0, part: int = 0) -> dict:
    streams_of = jax.random.split(jax.random.key(seed), 8)
    part_keys = jax.random.split(jax.random.fold_in(streams_of[7], part), 8)
    return {
        "pieces": bell_draw(part_keys[0], (2, MIDS, OFF), 1.0, 6.0, ((1, 8), (2, 2))),
        "destination": draw_destination(jax.random.fold_in(streams_of[7], 71), part),
        "first_offset": draw_first_offset(jax.random.fold_in(streams_of[7], 71), part),
        "valid_length": draw_valid_length(jax.random.fold_in(streams_of[7], 71), part),
        "midpoint_factor": bell_draw(part_keys[4], (MIDS, 2 * RANK), 0.05, 0.3, ((0, 8),), jnp.float32),
        "offset_factor": bell_draw(part_keys[5], (OFF, 2 * RANK), 1.0, 6.0, ((0, 2),), jnp.float32),
        "threshold": jnp.clip(jnp.exp(math.log(3.0) - 2.3025851 * jax.random.uniform(part_keys[6], (OFF,), jnp.float32) ** block_levels(part_keys[6], (OFF,), ((0, 2),), -0.2, 0.2)), 0.3, 3.0),
    }


epsilon = 1e-06

def reference(pieces, destination, first_offset, valid_length, midpoint_factor, offset_factor, threshold):
    total_rows = pieces.shape[1]
    col_total = pieces.shape[2]
    half_rank = midpoint_factor.shape[1] // 2
    block_total = total_rows // ROWS_DEV
    columns = jnp.arange(col_total, dtype=jnp.int32)
    left_factor = midpoint_factor
    right_factor = offset_factor
    sparse_blocks = None
    for sweep in range(ITERS):
        right_low = right_factor.astype(jnp.bfloat16)
        right_turn = jnp.concatenate([-right_factor[:, half_rank:], right_factor[:, :half_rank]], 1).astype(jnp.bfloat16)
        left_seg = left_factor.astype(jnp.bfloat16)[destination]
        left_turn = jnp.concatenate([left_seg[:, half_rank:], -left_seg[:, :half_rank]], 1)
        right_norm = lax.optimization_barrier(jnp.sum(right_factor[:, :half_rank] ** 2 + right_factor[:, half_rank:] ** 2, 0))
        left_norm = lax.optimization_barrier(jnp.sum(left_factor[:, :half_rank] ** 2 + left_factor[:, half_rank:] ** 2, 0))

        def one_block(offset_grad, block_index):
            first_row = block_index * ROWS_DEV
            observed = lax.dynamic_slice_in_dim(pieces, first_row, ROWS_DEV, 1).astype(jnp.float32)
            begin_col = lax.dynamic_slice_in_dim(first_offset, first_row, ROWS_DEV, 0)
            span_cols = lax.dynamic_slice_in_dim(valid_length, first_row, ROWS_DEV, 0)
            inside = (columns[None, :] >= begin_col[:, None]) & (columns[None, :] < (begin_col + span_cols)[:, None])
            row_factor = lax.dynamic_slice_in_dim(left_seg, first_row, ROWS_DEV, 0)
            row_turn = lax.dynamic_slice_in_dim(left_turn, first_row, ROWS_DEV, 0)
            model_real = jnp.dot(row_factor, right_low.T, preferred_element_type=jnp.float32)
            model_imag = jnp.dot(row_factor, right_turn.T, preferred_element_type=jnp.float32)
            resid_real = jnp.where(inside, observed[0] - model_real, jnp.float32(0.0))
            resid_imag = jnp.where(inside, observed[1] - model_imag, jnp.float32(0.0))
            magnitude = jnp.sqrt(resid_real * resid_real + resid_imag * resid_imag)
            factor = jnp.maximum(magnitude - threshold[None, :], 0.0) / jnp.maximum(magnitude, threshold[None, :])
            sparse_real = resid_real * factor
            sparse_imag = resid_imag * factor
            error_real = (resid_real - sparse_real).astype(jnp.bfloat16)
            error_imag = (resid_imag - sparse_imag).astype(jnp.bfloat16)
            row_grad = jnp.dot(error_real, right_low, preferred_element_type=jnp.float32) + jnp.dot(error_imag, right_turn, preferred_element_type=jnp.float32)
            offset_grad = offset_grad + jnp.dot(error_real.T, row_factor, preferred_element_type=jnp.float32) + jnp.dot(error_imag.T, row_turn, preferred_element_type=jnp.float32)
            return (offset_grad, (jnp.stack([sparse_real, sparse_imag]), row_grad))
        start_grad = jnp.zeros((col_total, 2 * half_rank), jnp.float32)
        offset_grad, (sparse_blocks, row_grads) = lax.scan(one_block, start_grad, jnp.arange(block_total, dtype=jnp.int32))
        row_grads = row_grads.reshape(total_rows, 2 * half_rank)
        row_step = row_grads / (jnp.concatenate([right_norm, right_norm]) + epsilon)
        left_next = left_factor + jnp.zeros_like(left_factor).at[destination].set(row_step)
        right_factor = right_factor + offset_grad / (jnp.concatenate([left_norm, left_norm]) + epsilon)
        left_factor = left_next
    sparse = jnp.transpose(sparse_blocks, (1, 0, 2, 3)).reshape(2, total_rows, col_total).astype(jnp.bfloat16)
    return (sparse, left_factor, right_factor)
```

```python
import functools

import jax
import jax.numpy as jnp
from jax import lax
from jax.experimental import pallas as pl
from jax.experimental.pallas import tpu as pltpu
from jax.sharding import PartitionSpec as P

ITERS = 2
CHUNKS = 8

epsilon = 1e-06
F32 = jnp.float32
BF16 = jnp.bfloat16
MESH = pl.DeviceIdType.MESH


def swap_halves(x):
    half = x.shape[1] // 2
    return jnp.concatenate([x[:, half:], x[:, :half]], 1)


def turned(x):
    half = x.shape[1] // 2
    return jnp.concatenate([x[:, half:], -x[:, :half]], 1)


def kernel(
    wide,
    chunk,
    pieces,
    dest,
    first,
    valid,
    u_in,
    v_in,
    thr,
    sp_out,
    u_out,
    v_out,
    v_low,
    acc,
    sent,
    got,
    total,
    stack,
    u_seg,
    row_acc,
    u_high,
    u_rest,
    own_high,
    own_rest,
    norm_own,
    norms,
    row_own,
    row_peer,
    step_own,
    steps,
    rs_send,
    rs_recv,
    ag_send,
    ag_recv,
    high_send,
    high_recv,
    rest_send,
    rest_recv,
    norm_send,
    norm_recv,
    row_send,
    row_recv,
    step_send,
    step_recv,
):
    g = lax.axis_index("groups")
    w = lax.axis_index("wide")
    n = lax.axis_index("narrow")
    rows, rank2 = u_in.shape
    cols = v_in.shape[0]
    chunks = cols // chunk
    bits = wide.bit_length() - 1
    peers = [lax.bitwise_xor(w, jnp.int32(j)) for j in range(1, wide)]
    side = 1 - n
    pending = []

    def send(src, dst, s_sem, r_sem, to_wide=None, to_narrow=None):
        copy = pltpu.make_async_remote_copy(
            src_ref=src,
            dst_ref=dst,
            send_sem=s_sem,
            recv_sem=r_sem,
            device_id=(g, w if to_wide is None else to_wide, n if to_narrow is None else to_narrow),
            device_id_type=MESH,
        )
        copy.start()
        pending.append(copy)
        return copy

    barrier = pltpu.get_barrier_semaphore()
    for p in peers:
        pl.semaphore_signal(barrier, inc=1, device_id=(g, p, n), device_id_type=MESH)
    pl.semaphore_signal(barrier, inc=1, device_id=(g, w, side), device_id_type=MESH)

    u0 = u_in[...]
    high = u0.astype(BF16)
    own_high[...] = high
    own_rest[...] = (u0 - high.astype(F32)).astype(BF16)
    u_high[w] = own_high[...]
    u_rest[w] = own_rest[...]
    part = jnp.broadcast_to(jnp.sum(u0 * u0, 0, keepdims=True), (8, rank2))
    norm_own[0] = part
    norms[0, w] = part
    pl.semaphore_wait(barrier, wide)

    waits = {}

    def gather(name, src, dst, s_sem, r_sem):
        for j, p in enumerate(peers):
            waits.setdefault(name, []).append(
                send(src, dst, s_sem.at[j], r_sem.at[j], to_wide=p)
            )

    def finish(name):
        for copy in waits[name]:
            copy.wait_recv()

    gather("high", own_high, u_high.at[w], high_send, high_recv)
    gather("norm0", norm_own.at[0], norms.at[0, w], norm_send.at[0], norm_recv.at[0])
    gather("rest", own_rest, u_rest.at[w], rest_send, rest_recv)

    eye = lax.broadcasted_iota(jnp.int32, (rows, rows), 0) == lax.broadcasted_iota(
        jnp.int32, (rows, rows), 1
    )

    def column(ref):
        wide_row = jnp.broadcast_to(ref[...].astype(F32), (rows, rows))
        return jnp.sum(jnp.where(eye, wide_row, 0.0), 1, keepdims=True).astype(jnp.int32)

    dest_col = column(dest)
    begin_col = column(first) - n * cols
    end_col = begin_col + column(valid)
    pick = (
        lax.broadcasted_iota(jnp.int32, (rows, wide * rows), 1) == dest_col
    ).astype(BF16)

    square = jnp.zeros((1, rank2), F32)
    for c in range(chunks):
        at = pl.ds(c * chunk, chunk)
        v = v_in[at]
        v_low[at] = v.astype(BF16)
        square = square + jnp.sum(v * v, 0, keepdims=True)
    squares = [square, jnp.zeros((1, rank2), F32)]

    def left_ready(value):
        low = value.astype(BF16)
        stack[:rows] = low
        stack[rows:] = turned(low.astype(F32)).astype(BF16)

    finish("high")
    picked_high = jnp.dot(
        pick, u_high[...].reshape(wide * rows, rank2), preferred_element_type=F32
    )
    left_ready(picked_high)

    def left_scale(it):
        finish("norm%d" % it)
        s = norms[it, 0, :1]
        for j in range(1, wide):
            s = s + norms[it, j, :1]
        return 1.0 / (s + swap_halves(s) + epsilon)

    scale = [None] * ITERS
    flights = {}

    def order(c):
        base = list(range(bits))
        if c % 2 and bits > 1:
            base[0], base[1] = base[1], base[0]
        return base

    def bit_of(b):
        return lax.bitwise_and(lax.shift_right_logical(w, jnp.int32(b)), 1)

    def place(c, s):
        start, size = jnp.int32(c * chunk), chunk
        for b in order(c)[:s]:
            size //= 2
            start = start + bit_of(b) * size
        return pl.multiple_of(start, size), size

    def scatter_send(it, c, s):
        b = order(c)[s]
        start, size = place(c, s)
        half = size // 2
        away = pl.ds(pl.multiple_of(start + (1 - bit_of(b)) * half, half), half)
        sent[it, away] = acc[away].astype(BF16)
        slot = chunk - size
        flights[it, c, s] = send(
            sent.at[it, away],
            got.at[it, c, pl.ds(slot, half)],
            rs_send.at[it, c, s],
            rs_recv.at[it, c, s],
            to_wide=lax.bitwise_xor(w, jnp.int32(1 << b)),
        )

    def scatter_take(it, c, s):
        flights[it, c, s].wait_recv()
        start, size = place(c, s + 1)
        mine = pl.ds(start, size)
        summed = acc[mine] + got[it, c, pl.ds(chunk - 2 * size, size)].astype(F32)
        if s == bits - 1:
            total[it, mine] = summed.astype(BF16)
        else:
            acc[mine] = summed

    def gather_send(it, c, s):
        start, size = place(c, s + 1)
        mine = pl.ds(start, size)
        flights[it, c, "g", s] = send(
            total.at[it, mine],
            total.at[it, mine],
            ag_send.at[it, c, s],
            ag_recv.at[it, c, s],
            to_wide=lax.bitwise_xor(w, jnp.int32(1 << order(c)[s])),
        )

    def compute(it, c):
        at = pl.ds(c * chunk, chunk)
        low = v_low[at]
        left = stack[...]
        model = lax.dot_general(left, low, (((1,), (1,)), ((), ())), preferred_element_type=F32)
        lane = lax.broadcasted_iota(jnp.int32, (rows, chunk), 1) + c * chunk
        inside = (lane >= begin_col) & (lane < end_col)
        real = jnp.where(inside, pieces[0, :, at].astype(F32) - model[:rows], 0.0)
        imag = jnp.where(inside, pieces[1, :, at].astype(F32) - model[rows:], 0.0)
        keep = jnp.minimum(thr[:, at] * lax.rsqrt(real * real + imag * imag), 1.0)
        err_real = real * keep
        err_imag = imag * keep
        if it == ITERS - 1:
            sp_out[0, :, at] = (real - err_real).astype(BF16)
            sp_out[1, :, at] = (imag - err_imag).astype(BF16)
        err = jnp.concatenate([err_real, err_imag], 0).astype(BF16)
        row = jnp.dot(err, low, preferred_element_type=F32)
        row_acc[...] = row if c == 0 else row_acc[...] + row
        acc[at] = lax.dot_general(err, left, (((0,), (0,)), ((), ())), preferred_element_type=F32)
        scatter_send(it, c, 0)

    def row_exchange(it):
        row = row_acc[...]
        row_own[it, :rows] = row[:rows] - turned(row[rows:])
        row_own[it, rows:] = jnp.broadcast_to(squares[it], (8, rank2))
        flights[it, "row"] = send(
            row_own.at[it], row_peer.at[it], row_send.at[it], row_recv.at[it], to_narrow=side
        )

    def row_step(it):
        flights[it, "row"].wait_recv()
        both = row_own[it] + row_peer[it]
        square = both[rows : rows + 1]
        return both[:rows] / (square + swap_halves(square) + epsilon)

    def update(it, c):
        at = pl.ds(c * chunk, chunk)
        if scale[it] is None:
            scale[it] = left_scale(it)
        source = v_in if it == 0 else v_out
        new = source[at] + total[it, at].astype(F32) * scale[it]
        v_out[at] = new
        if it < ITERS - 1:
            v_low[at] = new.astype(BF16)
            squares[it + 1] = squares[it + 1] + jnp.sum(new * new, 0, keepdims=True)

    def stage(it, c, s):
        if s == 0:
            compute(it, c)
        elif s <= bits:
            scatter_take(it, c, s - 1)
            if s < bits:
                scatter_send(it, c, s)
            else:
                gather_send(it, c, bits - 1)
        else:
            r = 2 * bits - s
            flights[it, c, "g", r].wait_recv()
            if r > 0:
                gather_send(it, c, r - 1)
            else:
                update(it, c)

    last = 2 * bits
    spacing = max(chunks, last)
    step_sum = None
    for t in range(spacing * (ITERS - 1) + chunks + last):
        for it in range(ITERS):
            local_t = t - it * spacing
            if it > 0 and local_t == 0:
                step = row_step(it - 1)
                if it == 1:
                    finish("rest")
                    u_seg[...] = picked_high + jnp.dot(
                        pick,
                        u_rest[...].reshape(wide * rows, rank2),
                        preferred_element_type=F32,
                    )
                step_sum = step if step_sum is None else step_sum + step
                value = u_seg[...] + step
                u_seg[...] = value
                left_ready(value)
                part = jnp.broadcast_to(jnp.sum(value * value, 0, keepdims=True), (8, rank2))
                norm_own[it] = part
                norms[it, w] = part
                gather(
                    "norm%d" % it,
                    norm_own.at[it],
                    norms.at[it, w],
                    norm_send.at[it],
                    norm_recv.at[it],
                )
            for s in range(last, -1, -1):
                c = local_t - s
                if 0 <= c < chunks:
                    stage(it, c, s)
                    if s == 0 and c == chunks - 1:
                        row_exchange(it)
        if t == spacing * (ITERS - 1) + chunks:
            step_sum = step_sum + row_step(ITERS - 1)
            spread = (
                lax.broadcasted_iota(jnp.int32, (wide * rows, rows), 0)
                == jnp.broadcast_to(dest[...], (wide * rows, rows))
            ).astype(BF16)
            placed = jnp.dot(spread, step_sum.astype(BF16), preferred_element_type=F32)
            step_own[...] = placed.astype(BF16).reshape(wide, rows, rank2)
            steps[w] = step_own[w]
            for j, p in enumerate(peers):
                waits.setdefault("step", []).append(
                    send(
                        step_own.at[p], steps.at[w], step_send.at[j], step_recv.at[j], to_wide=p
                    )
                )
    finish("step")
    out = u_in[...]
    for j in range(wide):
        out = out + steps[j].astype(F32)
    u_out[...] = out
    for copy in pending:
        copy.wait_send()


def local(
    pieces, destination, first_offset, valid_length, midpoint_factor, offset_factor, threshold
):
    wide = lax.axis_size("wide")
    rows, rank2 = midpoint_factor.shape
    cols = offset_factor.shape[0]
    chunk = max(cols // CHUNKS, 16 * wide)
    chunks = cols // chunk
    bits = wide.bit_length() - 1
    vmem = pl.BlockSpec(memory_space=pltpu.VMEM)
    dma = pltpu.SemaphoreType.DMA
    return pl.pallas_call(
        functools.partial(kernel, wide, chunk),
        out_shape=(
            jax.ShapeDtypeStruct(pieces.shape, BF16),
            jax.ShapeDtypeStruct(midpoint_factor.shape, F32),
            jax.ShapeDtypeStruct(offset_factor.shape, F32),
        ),
        in_specs=[vmem] * 7,
        out_specs=(vmem,) * 3,
        scratch_shapes=[
            pltpu.VMEM((cols, rank2), BF16),
            pltpu.VMEM((cols, rank2), F32),
            pltpu.VMEM((ITERS, cols, rank2), BF16),
            pltpu.VMEM((ITERS, chunks, chunk, rank2), BF16),
            pltpu.VMEM((ITERS, cols, rank2), BF16),
            pltpu.VMEM((2 * rows, rank2), BF16),
            pltpu.VMEM((rows, rank2), F32),
            pltpu.VMEM((2 * rows, rank2), F32),
            pltpu.VMEM((wide, rows, rank2), BF16),
            pltpu.VMEM((wide, rows, rank2), BF16),
            pltpu.VMEM((rows, rank2), BF16),
            pltpu.VMEM((rows, rank2), BF16),
            pltpu.VMEM((ITERS, 8, rank2), F32),
            pltpu.VMEM((ITERS, wide, 8, rank2), F32),
            pltpu.VMEM((ITERS, rows + 8, rank2), F32),
            pltpu.VMEM((ITERS, rows + 8, rank2), F32),
            pltpu.VMEM((wide, rows, rank2), BF16),
            pltpu.VMEM((wide, rows, rank2), BF16),
            dma((ITERS, chunks, bits)),
            dma((ITERS, chunks, bits)),
            dma((ITERS, chunks, bits)),
            dma((ITERS, chunks, bits)),
            dma((wide - 1,)),
            dma((wide - 1,)),
            dma((wide - 1,)),
            dma((wide - 1,)),
            dma((ITERS, wide - 1)),
            dma((ITERS, wide - 1)),
            dma((ITERS,)),
            dma((ITERS,)),
            dma((wide - 1,)),
            dma((wide - 1,)),
        ],
        compiler_params=pltpu.CompilerParams(
            collective_id=0, has_side_effects=True, vmem_limit_bytes=48 * 1024 * 1024
        ),
        cost_estimate=pl.CostEstimate(
            flops=ITERS * 3 * 4 * rows * rank2 * cols,
            bytes_accessed=12 * cols * rank2,
            transcendentals=0,
        ),
    )(
        pieces,
        destination.reshape(1, rows),
        first_offset.reshape(1, rows),
        valid_length.reshape(1, rows),
        midpoint_factor,
        offset_factor,
        threshold.reshape(1, cols),
    )


def solution(mesh):
    placed = (
        P(None, ("groups", "wide"), "narrow"),
        P("wide"),
        P("wide"),
        P("wide"),
        P(("groups", "wide"), None),
        P(("groups", "narrow"), None),
        P(("groups", "narrow")),
    )
    return jax.shard_map(
        local,
        mesh=mesh,
        in_specs=placed,
        out_specs=(
            P(None, ("groups", "wide"), "narrow"),
            P(("groups", "wide"), None),
            P(("groups", "narrow"), None),
        ),
        check_vma=False,
    )
```

```python
import functools

import jax
import jax.numpy as jnp
from jax import lax
from jax.experimental import pallas as pl
from jax.experimental.pallas import tpu as pltpu
from jax.sharding import PartitionSpec as P

ITERS = 2
CHUNKS = 8
GAP = 3

epsilon = 1e-06
F32 = jnp.float32
BF16 = jnp.bfloat16
MESH = pl.DeviceIdType.MESH


def swap_halves(x):
    half = x.shape[1] // 2
    return jnp.concatenate([x[:, half:], x[:, :half]], 1)


def turned(x):
    half = x.shape[1] // 2
    return jnp.concatenate([x[:, half:], -x[:, :half]], 1)


def kernel(
    wide,
    chunk,
    pieces_hbm,
    dest_hbm,
    first_hbm,
    valid_hbm,
    u_hbm,
    v_hbm,
    thr_hbm,
    sp_hbm,
    u_out,
    v_out_hbm,
    pieces,
    dest,
    first,
    valid,
    u_in,
    v_now,
    thr,
    in_sem,
    out_sem,
    v_low,
    acc,
    sent,
    got,
    total,
    stack,
    u_seg,
    row_acc,
    u_high,
    u_rest,
    own_high,
    own_rest,
    norm_own,
    norms,
    row_own,
    row_peer,
    step_own,
    steps,
    rs_send,
    rs_recv,
    ag_send,
    ag_recv,
    high_send,
    high_recv,
    rest_send,
    rest_recv,
    norm_send,
    norm_recv,
    row_send,
    row_recv,
    step_send,
    step_recv,
):
    g = lax.axis_index("groups")
    w = lax.axis_index("wide")
    n = lax.axis_index("narrow")
    rows, rank2 = u_in.shape
    cols = v_now.shape[0]
    chunks = cols // chunk
    bits = wide.bit_length() - 1
    peers = [lax.bitwise_xor(w, jnp.int32(j)) for j in range(1, wide)]
    side = 1 - n
    pending = []
    loads = [
        pltpu.make_async_copy(src, dst, in_sem.at[i])
        for i, (src, dst) in enumerate(
            [
                (u_hbm, u_in),
                (dest_hbm, dest),
                (first_hbm, first),
                (valid_hbm, valid),
                (v_hbm, v_now),
                (thr_hbm, thr),
                (pieces_hbm, pieces),
            ]
        )
    ]
    for load in loads:
        load.start()
    stores = []

    def store(src, dst, sem):
        copy = pltpu.make_async_copy(src, dst, sem)
        copy.start()
        stores.append(copy)

    def send(src, dst, s_sem, r_sem, to_wide=None, to_narrow=None):
        copy = pltpu.make_async_remote_copy(
            src_ref=src,
            dst_ref=dst,
            send_sem=s_sem,
            recv_sem=r_sem,
            device_id=(g, w if to_wide is None else to_wide, n if to_narrow is None else to_narrow),
            device_id_type=MESH,
        )
        copy.start()
        pending.append(copy)
        return copy

    barrier = pltpu.get_barrier_semaphore()
    for p in peers:
        pl.semaphore_signal(barrier, inc=1, device_id=(g, p, n), device_id_type=MESH)
    pl.semaphore_signal(barrier, inc=1, device_id=(g, w, side), device_id_type=MESH)

    loads[0].wait()
    u0 = u_in[...]
    high = u0.astype(BF16)
    own_high[...] = high
    own_rest[...] = (u0 - high.astype(F32)).astype(BF16)
    u_high[w] = own_high[...]
    u_rest[w] = own_rest[...]
    part = jnp.broadcast_to(jnp.sum(u0 * u0, 0, keepdims=True), (8, rank2))
    norm_own[0] = part
    norms[0, w] = part
    pl.semaphore_wait(barrier, wide)

    waits = {}

    def gather(name, src, dst, s_sem, r_sem):
        for j, p in enumerate(peers):
            waits.setdefault(name, []).append(
                send(src, dst, s_sem.at[j], r_sem.at[j], to_wide=p)
            )

    def finish(name):
        for copy in waits[name]:
            copy.wait_recv()

    gather("high", own_high, u_high.at[w], high_send, high_recv)
    gather("norm0", norm_own.at[0], norms.at[0, w], norm_send.at[0], norm_recv.at[0])

    for load in loads[1:5]:
        load.wait()
    eye = lax.broadcasted_iota(jnp.int32, (rows, rows), 0) == lax.broadcasted_iota(
        jnp.int32, (rows, rows), 1
    )

    def column(ref):
        wide_row = jnp.broadcast_to(ref[...].astype(F32), (rows, rows))
        return jnp.sum(jnp.where(eye, wide_row, 0.0), 1, keepdims=True).astype(jnp.int32)

    dest_col = column(dest)
    begin_col = column(first) - n * cols
    end_col = begin_col + column(valid)
    pick = (
        lax.broadcasted_iota(jnp.int32, (rows, wide * rows), 1) == dest_col
    ).astype(BF16)

    square = jnp.zeros((1, rank2), F32)
    for c in range(chunks):
        at = pl.ds(c * chunk, chunk)
        v = v_now[at]
        v_low[at] = v.astype(BF16)
        square = square + jnp.sum(v * v, 0, keepdims=True)
    squares = [square, jnp.zeros((1, rank2), F32)]

    def left_ready(value):
        low = value.astype(BF16)
        stack[:rows] = low
        stack[rows:] = turned(low.astype(F32)).astype(BF16)

    for load in loads[5:]:
        load.wait()
    finish("high")
    picked_high = jnp.dot(
        pick, u_high[...].reshape(wide * rows, rank2), preferred_element_type=F32
    )
    left_ready(picked_high)

    def left_scale(it):
        finish("norm%d" % it)
        s = norms[it, 0, :1]
        for j in range(1, wide):
            s = s + norms[it, j, :1]
        return 1.0 / (s + swap_halves(s) + epsilon)

    scale = [None] * ITERS
    flights = {}

    def order(c):
        base = list(range(bits))
        if c % 2 and bits > 1:
            base[0], base[1] = base[1], base[0]
        return base

    def bit_of(b):
        return lax.bitwise_and(lax.shift_right_logical(w, jnp.int32(b)), 1)

    def place(c, s):
        start, size = jnp.int32(c * chunk), chunk
        for b in order(c)[:s]:
            size //= 2
            start = start + bit_of(b) * size
        return pl.multiple_of(start, size), size

    def scatter_send(it, c, s):
        b = order(c)[s]
        start, size = place(c, s)
        half = size // 2
        away = pl.ds(pl.multiple_of(start + (1 - bit_of(b)) * half, half), half)
        sent[it, away] = acc[away].astype(BF16)
        slot = chunk - size
        flights[it, c, s] = send(
            sent.at[it, away],
            got.at[it, c, pl.ds(slot, half)],
            rs_send.at[it, c, s],
            rs_recv.at[it, c, s],
            to_wide=lax.bitwise_xor(w, jnp.int32(1 << b)),
        )

    def scatter_take(it, c, s):
        flights[it, c, s].wait_recv()
        start, size = place(c, s + 1)
        mine = pl.ds(start, size)
        summed = acc[mine] + got[it, c, pl.ds(chunk - 2 * size, size)].astype(F32)
        if s == bits - 1:
            total[it, mine] = summed.astype(BF16)
        else:
            acc[mine] = summed

    def gather_send(it, c, s):
        start, size = place(c, s + 1)
        mine = pl.ds(start, size)
        flights[it, c, "g", s] = send(
            total.at[it, mine],
            total.at[it, mine],
            ag_send.at[it, c, s],
            ag_recv.at[it, c, s],
            to_wide=lax.bitwise_xor(w, jnp.int32(1 << order(c)[s])),
        )

    def compute(it, c):
        at = pl.ds(c * chunk, chunk)
        low = v_low[at]
        left = stack[...]
        model = lax.dot_general(left, low, (((1,), (1,)), ((), ())), preferred_element_type=F32)
        lane = lax.broadcasted_iota(jnp.int32, (rows, chunk), 1) + c * chunk
        inside = (lane >= begin_col) & (lane < end_col)
        real = jnp.where(inside, pieces[0, :, at].astype(F32) - model[:rows], 0.0)
        imag = jnp.where(inside, pieces[1, :, at].astype(F32) - model[rows:], 0.0)
        keep = jnp.minimum(thr[:, at] * lax.rsqrt(real * real + imag * imag), 1.0)
        err_real = real * keep
        err_imag = imag * keep
        if it == ITERS - 1:
            pieces[0, :, at] = (real - err_real).astype(BF16)
            pieces[1, :, at] = (imag - err_imag).astype(BF16)
            store(pieces.at[:, :, at], sp_hbm.at[:, :, at], out_sem.at[0, c])
        err = jnp.concatenate([err_real, err_imag], 0).astype(BF16)
        row = jnp.dot(err, low, preferred_element_type=F32)
        row_acc[...] = row if c == 0 else row_acc[...] + row
        acc[at] = lax.dot_general(err, left, (((0,), (0,)), ((), ())), preferred_element_type=F32)
        scatter_send(it, c, 0)

    def row_exchange(it):
        row = row_acc[...]
        row_own[it, :rows] = row[:rows] - turned(row[rows:])
        row_own[it, rows:] = jnp.broadcast_to(squares[it], (8, rank2))
        flights[it, "row"] = send(
            row_own.at[it], row_peer.at[it], row_send.at[it], row_recv.at[it], to_narrow=side
        )

    def row_step(it):
        flights[it, "row"].wait_recv()
        both = row_own[it] + row_peer[it]
        square = both[rows : rows + 1]
        return both[:rows] / (square + swap_halves(square) + epsilon)

    def update(it, c):
        at = pl.ds(c * chunk, chunk)
        if scale[it] is None:
            scale[it] = left_scale(it)
        new = v_now[at] + total[it, at].astype(F32) * scale[it]
        v_now[at] = new
        if it < ITERS - 1:
            v_low[at] = new.astype(BF16)
            squares[it + 1] = squares[it + 1] + jnp.sum(new * new, 0, keepdims=True)
        else:
            store(v_now.at[at], v_out_hbm.at[at], out_sem.at[1, c])

    def stage(it, c, s):
        if s == 0:
            compute(it, c)
        elif s <= bits:
            scatter_take(it, c, s - 1)
            if s < bits:
                scatter_send(it, c, s)
            else:
                gather_send(it, c, bits - 1)
        else:
            r = 2 * bits - s
            flights[it, c, "g", r].wait_recv()
            if r > 0:
                gather_send(it, c, r - 1)
            else:
                update(it, c)

    def left_update(it):
        step = row_step(it - 1)
        if it == 1:
            finish("rest")
            u_seg[...] = picked_high + jnp.dot(
                pick, u_rest[...].reshape(wide * rows, rank2), preferred_element_type=F32
            )
        value = u_seg[...] + step
        u_seg[...] = value
        left_ready(value)
        part = jnp.broadcast_to(jnp.sum(value * value, 0, keepdims=True), (8, rank2))
        norm_own[it] = part
        norms[it, w] = part
        gather(
            "norm%d" % it, norm_own.at[it], norms.at[it, w], norm_send.at[it], norm_recv.at[it]
        )
        return step

    def step_exchange(step_sum):
        spread = (
            lax.broadcasted_iota(jnp.int32, (wide * rows, rows), 0)
            == jnp.broadcast_to(dest[...], (wide * rows, rows))
        ).astype(BF16)
        placed = jnp.dot(spread, step_sum.astype(BF16), preferred_element_type=F32)
        step_own[...] = placed.astype(BF16).reshape(wide, rows, rank2)
        steps[w] = step_own[w]
        for j, p in enumerate(peers):
            waits.setdefault("step", []).append(
                send(step_own.at[p], steps.at[w], step_send.at[j], step_recv.at[j], to_wide=p)
            )

    last = 2 * bits
    spacing = max(chunks, GAP * last)
    events = []
    for it in range(ITERS):
        for c in range(chunks):
            for s in range(last + 1):
                events.append((it * spacing + c + GAP * s, it, -s, "stage", c))
        events.append((it * spacing + chunks - 1, it, 1, "exchange", 0))
        events.append((min(it * spacing + chunks - 1 + GAP, (it + 1) * spacing), it, 2, "step", 0))
    events.append((1, 0, 3, "rest", 0))
    step_sum = None
    for _, it, s, what, c in sorted(events):
        if what == "stage":
            stage(it, c, -s)
        elif what == "exchange":
            row_exchange(it)
        elif what == "rest":
            gather("rest", own_rest, u_rest.at[w], rest_send, rest_recv)
        else:
            step = left_update(it + 1) if it + 1 < ITERS else row_step(it)
            step_sum = step if step_sum is None else step_sum + step
            if it + 1 == ITERS:
                step_exchange(step_sum)
    finish("step")
    out = u_in[...]
    for j in range(wide):
        out = out + steps[j].astype(F32)
    u_out[...] = out
    for copy in pending:
        copy.wait_send()
    for copy in stores:
        copy.wait()


def local(
    pieces, destination, first_offset, valid_length, midpoint_factor, offset_factor, threshold
):
    wide = lax.axis_size("wide")
    rows, rank2 = midpoint_factor.shape
    cols = offset_factor.shape[0]
    chunk = max(cols // CHUNKS, 16 * wide)
    chunks = cols // chunk
    bits = wide.bit_length() - 1
    vmem = pl.BlockSpec(memory_space=pltpu.VMEM)
    hbm = pl.BlockSpec(memory_space=pl.ANY)
    dma = pltpu.SemaphoreType.DMA
    return pl.pallas_call(
        functools.partial(kernel, wide, chunk),
        out_shape=(
            jax.ShapeDtypeStruct(pieces.shape, BF16),
            jax.ShapeDtypeStruct(midpoint_factor.shape, F32),
            jax.ShapeDtypeStruct(offset_factor.shape, F32),
        ),
        in_specs=[hbm] * 7,
        out_specs=(hbm, vmem, hbm),
        scratch_shapes=[
            pltpu.VMEM(pieces.shape, BF16),
            pltpu.VMEM((1, rows), jnp.int32),
            pltpu.VMEM((1, rows), jnp.int32),
            pltpu.VMEM((1, rows), jnp.int32),
            pltpu.VMEM((rows, rank2), F32),
            pltpu.VMEM((cols, rank2), F32),
            pltpu.VMEM((1, cols), F32),
            dma((7,)),
            dma((2, chunks)),
            pltpu.VMEM((cols, rank2), BF16),
            pltpu.VMEM((cols, rank2), F32),
            pltpu.VMEM((ITERS, cols, rank2), BF16),
            pltpu.VMEM((ITERS, chunks, chunk, rank2), BF16),
            pltpu.VMEM((ITERS, cols, rank2), BF16),
            pltpu.VMEM((2 * rows, rank2), BF16),
            pltpu.VMEM((rows, rank2), F32),
            pltpu.VMEM((2 * rows, rank2), F32),
            pltpu.VMEM((wide, rows, rank2), BF16),
            pltpu.VMEM((wide, rows, rank2), BF16),
            pltpu.VMEM((rows, rank2), BF16),
            pltpu.VMEM((rows, rank2), BF16),
            pltpu.VMEM((ITERS, 8, rank2), F32),
            pltpu.VMEM((ITERS, wide, 8, rank2), F32),
            pltpu.VMEM((ITERS, rows + 8, rank2), F32),
            pltpu.VMEM((ITERS, rows + 8, rank2), F32),
            pltpu.VMEM((wide, rows, rank2), BF16),
            pltpu.VMEM((wide, rows, rank2), BF16),
            dma((ITERS, chunks, bits)),
            dma((ITERS, chunks, bits)),
            dma((ITERS, chunks, bits)),
            dma((ITERS, chunks, bits)),
            dma((wide - 1,)),
            dma((wide - 1,)),
            dma((wide - 1,)),
            dma((wide - 1,)),
            dma((ITERS, wide - 1)),
            dma((ITERS, wide - 1)),
            dma((ITERS,)),
            dma((ITERS,)),
            dma((wide - 1,)),
            dma((wide - 1,)),
        ],
        compiler_params=pltpu.CompilerParams(
            collective_id=0, has_side_effects=True, vmem_limit_bytes=56 * 1024 * 1024
        ),
        cost_estimate=pl.CostEstimate(
            flops=ITERS * 3 * 4 * rows * rank2 * cols,
            bytes_accessed=12 * cols * rank2,
            transcendentals=0,
        ),
    )(
        pieces,
        destination.reshape(1, rows),
        first_offset.reshape(1, rows),
        valid_length.reshape(1, rows),
        midpoint_factor,
        offset_factor,
        threshold.reshape(1, cols),
    )


def solution(mesh):
    placed = (
        P(None, ("groups", "wide"), "narrow"),
        P("wide"),
        P("wide"),
        P("wide"),
        P(("groups", "wide"), None),
        P(("groups", "narrow"), None),
        P(("groups", "narrow")),
    )
    return jax.shard_map(
        local,
        mesh=mesh,
        in_specs=placed,
        out_specs=(
            P(None, ("groups", "wide"), "narrow"),
            P(("groups", "wide"), None),
            P(("groups", "narrow"), None),
        ),
        check_vma=False,
    )
```

```python
import functools

import jax
import jax.numpy as jnp
from jax import lax
from jax.experimental import pallas as pl
from jax.experimental.pallas import tpu as pltpu
from jax.sharding import PartitionSpec as P

ITERS = 2
CHUNKS = 16

epsilon = 1e-06
F32 = jnp.float32
BF16 = jnp.bfloat16
MESH = pl.DeviceIdType.MESH


def order_of(c, bits):
    base = list(range(bits))
    if c % 2 and bits > 1:
        base[0], base[1] = base[1], base[0]
    return base


def plan(chunks, chunk, bits):
    delay, rate, work, step = 2.0, 45e3, 1.1 * chunk / 512, 0.1
    last = 2 * bits
    now, busy, arrived, order = 0.0, [0.0] * bits, {}, []
    stage_at = {(it, c): 0 for it in range(ITERS) for c in range(chunks)}
    computed, row_sent, row_done = [0] * ITERS, [None] * ITERS, [False] * ITERS
    while True:
        ready = []
        for (it, c), s in stage_at.items():
            if s == 0:
                allowed = it == 0 or (row_done[it - 1] and stage_at[it - 1, c] > last)
                if c == computed[it] and allowed:
                    ready.append((now, it, c, s))
            elif s <= last:
                ready.append((arrived[it, c], it, c, s))
        for it in range(ITERS):
            if row_sent[it] is not None and not row_done[it]:
                ready.append((row_sent[it] + delay, it, -1, 0))
        if not ready:
            return order
        when, it, c, s = min(ready)
        now = max(now, when)
        order.append((it, c, s))
        if c < 0:
            row_done[it] = True
            now += 0.5
            continue
        now += work if s == 0 else step + 0.2 * chunk / 512
        if s == 0:
            computed[it] += 1
            if computed[it] == chunks:
                row_sent[it] = now
        if s < last:
            r = s if s < bits else last - 1 - s
            b = order_of(c, bits)[r]
            start = max(busy[b], now)
            busy[b] = start + (chunk * 256 >> (r + 1)) / (rate if b < 2 else rate / 2)
            arrived[it, c] = busy[b] + delay
        stage_at[it, c] += 1


def swap_halves(x):
    half = x.shape[1] // 2
    return jnp.concatenate([x[:, half:], x[:, :half]], 1)


def turned(x):
    half = x.shape[1] // 2
    return jnp.concatenate([x[:, half:], -x[:, :half]], 1)


def kernel(
    wide,
    chunk,
    pieces_hbm,
    dest_hbm,
    first_hbm,
    valid_hbm,
    u_hbm,
    v_hbm,
    thr_hbm,
    sp_hbm,
    u_out,
    v_out_hbm,
    pieces,
    dest,
    first,
    valid,
    u_in,
    v_now,
    thr,
    in_sem,
    out_sem,
    v_low,
    acc,
    sent,
    got,
    total,
    stack,
    u_seg,
    row_acc,
    u_high,
    u_rest,
    own_high,
    own_rest,
    norm_own,
    norms,
    row_own,
    row_peer,
    step_own,
    steps,
    rs_send,
    rs_recv,
    ag_send,
    ag_recv,
    high_send,
    high_recv,
    rest_send,
    rest_recv,
    norm_send,
    norm_recv,
    row_send,
    row_recv,
    step_send,
    step_recv,
):
    g = lax.axis_index("groups")
    w = lax.axis_index("wide")
    n = lax.axis_index("narrow")
    rows, rank2 = u_in.shape
    cols = v_now.shape[0]
    chunks = cols // chunk
    bits = wide.bit_length() - 1
    peers = [lax.bitwise_xor(w, jnp.int32(j)) for j in range(1, wide)]
    side = 1 - n
    pending = []
    loads = [
        pltpu.make_async_copy(src, dst, in_sem.at[i])
        for i, (src, dst) in enumerate(
            [
                (u_hbm, u_in),
                (dest_hbm, dest),
                (first_hbm, first),
                (valid_hbm, valid),
                (v_hbm, v_now),
                (thr_hbm, thr),
                (pieces_hbm, pieces),
            ]
        )
    ]
    for load in loads:
        load.start()
    stores = []

    def store(src, dst, sem):
        copy = pltpu.make_async_copy(src, dst, sem)
        copy.start()
        stores.append(copy)

    def send(src, dst, s_sem, r_sem, to_wide=None, to_narrow=None):
        copy = pltpu.make_async_remote_copy(
            src_ref=src,
            dst_ref=dst,
            send_sem=s_sem,
            recv_sem=r_sem,
            device_id=(g, w if to_wide is None else to_wide, n if to_narrow is None else to_narrow),
            device_id_type=MESH,
        )
        copy.start()
        pending.append(copy)
        return copy

    barrier = pltpu.get_barrier_semaphore()
    for p in peers:
        pl.semaphore_signal(barrier, inc=1, device_id=(g, p, n), device_id_type=MESH)
    pl.semaphore_signal(barrier, inc=1, device_id=(g, w, side), device_id_type=MESH)

    loads[0].wait()
    u0 = u_in[...]
    high = u0.astype(BF16)
    own_high[...] = high
    own_rest[...] = (u0 - high.astype(F32)).astype(BF16)
    u_high[w] = own_high[...]
    u_rest[w] = own_rest[...]
    part = jnp.broadcast_to(jnp.sum(u0 * u0, 0, keepdims=True), (8, rank2))
    norm_own[0] = part
    norms[0, w] = part
    pl.semaphore_wait(barrier, wide)

    waits = {}

    def gather(name, src, dst, s_sem, r_sem):
        for j, p in enumerate(peers):
            waits.setdefault(name, []).append(
                send(src, dst, s_sem.at[j], r_sem.at[j], to_wide=p)
            )

    def finish(name):
        for copy in waits[name]:
            copy.wait_recv()

    gather("high", own_high, u_high.at[w], high_send, high_recv)
    gather("norm0", norm_own.at[0], norms.at[0, w], norm_send.at[0], norm_recv.at[0])

    for load in loads[1:5]:
        load.wait()
    eye = lax.broadcasted_iota(jnp.int32, (rows, rows), 0) == lax.broadcasted_iota(
        jnp.int32, (rows, rows), 1
    )

    def column(ref):
        wide_row = jnp.broadcast_to(ref[...].astype(F32), (rows, rows))
        return jnp.sum(jnp.where(eye, wide_row, 0.0), 1, keepdims=True).astype(jnp.int32)

    dest_col = column(dest)
    begin_col = column(first) - n * cols
    end_col = begin_col + column(valid)
    pick = (
        lax.broadcasted_iota(jnp.int32, (rows, wide * rows), 1) == dest_col
    ).astype(BF16)

    square = jnp.zeros((1, rank2), F32)
    for c in range(chunks):
        at = pl.ds(c * chunk, chunk)
        v = v_now[at]
        v_low[at] = v.astype(BF16)
        square = square + jnp.sum(v * v, 0, keepdims=True)
    squares = [square, jnp.zeros((1, rank2), F32)]

    def left_ready(value):
        low = value.astype(BF16)
        stack[:rows] = low
        stack[rows:] = turned(low.astype(F32)).astype(BF16)

    for load in loads[5:]:
        load.wait()
    finish("high")
    picked_high = jnp.dot(
        pick, u_high[...].reshape(wide * rows, rank2), preferred_element_type=F32
    )
    left_ready(picked_high)

    def left_scale(it):
        finish("norm%d" % it)
        s = norms[it, 0, :1]
        for j in range(1, wide):
            s = s + norms[it, j, :1]
        return 1.0 / (s + swap_halves(s) + epsilon)

    scale = [None] * ITERS
    flights = {}

    def bit_of(b):
        return lax.bitwise_and(lax.shift_right_logical(w, jnp.int32(b)), 1)

    def place(c, s):
        start, size = jnp.int32(c * chunk), chunk
        for b in order_of(c, bits)[:s]:
            size //= 2
            start = start + bit_of(b) * size
        return pl.multiple_of(start, size), size

    def scatter_send(it, c, s):
        b = order_of(c, bits)[s]
        start, size = place(c, s)
        half = size // 2
        away = pl.ds(pl.multiple_of(start + (1 - bit_of(b)) * half, half), half)
        sent[it, away] = acc[away].astype(BF16)
        slot = chunk - size
        flights[it, c, s] = send(
            sent.at[it, away],
            got.at[it, c, pl.ds(slot, half)],
            rs_send.at[it, c, s],
            rs_recv.at[it, c, s],
            to_wide=lax.bitwise_xor(w, jnp.int32(1 << b)),
        )

    def scatter_take(it, c, s):
        flights[it, c, s].wait_recv()
        start, size = place(c, s + 1)
        mine = pl.ds(start, size)
        summed = acc[mine] + got[it, c, pl.ds(chunk - 2 * size, size)].astype(F32)
        if s == bits - 1:
            total[it, mine] = summed.astype(BF16)
        else:
            acc[mine] = summed

    def gather_send(it, c, s):
        start, size = place(c, s + 1)
        mine = pl.ds(start, size)
        flights[it, c, "g", s] = send(
            total.at[it, mine],
            total.at[it, mine],
            ag_send.at[it, c, s],
            ag_recv.at[it, c, s],
            to_wide=lax.bitwise_xor(w, jnp.int32(1 << order_of(c, bits)[s])),
        )

    def compute(it, c):
        at = pl.ds(c * chunk, chunk)
        low = v_low[at]
        left = stack[...]
        model = lax.dot_general(left, low, (((1,), (1,)), ((), ())), preferred_element_type=F32)
        lane = lax.broadcasted_iota(jnp.int32, (rows, chunk), 1) + c * chunk
        inside = (lane >= begin_col) & (lane < end_col)
        real = jnp.where(inside, pieces[0, :, at].astype(F32) - model[:rows], 0.0)
        imag = jnp.where(inside, pieces[1, :, at].astype(F32) - model[rows:], 0.0)
        keep = jnp.minimum(thr[:, at] * lax.rsqrt(real * real + imag * imag), 1.0)
        err_real = real * keep
        err_imag = imag * keep
        if it == ITERS - 1:
            pieces[0, :, at] = (real - err_real).astype(BF16)
            pieces[1, :, at] = (imag - err_imag).astype(BF16)
            store(pieces.at[:, :, at], sp_hbm.at[:, :, at], out_sem.at[0, c])
        err = jnp.concatenate([err_real, err_imag], 0).astype(BF16)
        row = jnp.dot(err, low, preferred_element_type=F32)
        row_acc[...] = row if c == 0 else row_acc[...] + row
        acc[at] = lax.dot_general(err, left, (((0,), (0,)), ((), ())), preferred_element_type=F32)
        scatter_send(it, c, 0)

    def row_exchange(it):
        row = row_acc[...]
        row_own[it, :rows] = row[:rows] - turned(row[rows:])
        row_own[it, rows:] = jnp.broadcast_to(squares[it], (8, rank2))
        flights[it, "row"] = send(
            row_own.at[it], row_peer.at[it], row_send.at[it], row_recv.at[it], to_narrow=side
        )

    def row_step(it):
        flights[it, "row"].wait_recv()
        both = row_own[it] + row_peer[it]
        square = both[rows : rows + 1]
        return both[:rows] / (square + swap_halves(square) + epsilon)

    def update(it, c):
        at = pl.ds(c * chunk, chunk)
        if scale[it] is None:
            scale[it] = left_scale(it)
        new = v_now[at] + total[it, at].astype(F32) * scale[it]
        v_now[at] = new
        if it < ITERS - 1:
            v_low[at] = new.astype(BF16)
            squares[it + 1] = squares[it + 1] + jnp.sum(new * new, 0, keepdims=True)
        else:
            store(v_now.at[at], v_out_hbm.at[at], out_sem.at[1, c])

    def stage(it, c, s):
        if s == 0:
            compute(it, c)
        elif s <= bits:
            scatter_take(it, c, s - 1)
            if s < bits:
                scatter_send(it, c, s)
            else:
                gather_send(it, c, bits - 1)
        else:
            r = 2 * bits - s
            flights[it, c, "g", r].wait_recv()
            if r > 0:
                gather_send(it, c, r - 1)
            else:
                update(it, c)

    def left_update(it):
        step = row_step(it - 1)
        if it == 1:
            finish("rest")
            u_seg[...] = picked_high + jnp.dot(
                pick, u_rest[...].reshape(wide * rows, rank2), preferred_element_type=F32
            )
        value = u_seg[...] + step
        u_seg[...] = value
        left_ready(value)
        part = jnp.broadcast_to(jnp.sum(value * value, 0, keepdims=True), (8, rank2))
        norm_own[it] = part
        norms[it, w] = part
        gather(
            "norm%d" % it, norm_own.at[it], norms.at[it, w], norm_send.at[it], norm_recv.at[it]
        )
        return step

    def step_exchange(step_sum):
        spread = (
            lax.broadcasted_iota(jnp.int32, (wide * rows, rows), 0)
            == jnp.broadcast_to(dest[...], (wide * rows, rows))
        ).astype(BF16)
        placed = jnp.dot(spread, step_sum.astype(BF16), preferred_element_type=F32)
        step_own[...] = placed.astype(BF16).reshape(wide, rows, rank2)
        steps[w] = step_own[w]
        for j, p in enumerate(peers):
            waits.setdefault("step", []).append(
                send(step_own.at[p], steps.at[w], step_send.at[j], step_recv.at[j], to_wide=p)
            )

    last = 2 * bits
    step_sum = None
    for index, (it, c, s) in enumerate(plan(chunks, chunk, bits)):
        if index == min(2, chunks - 1):
            gather("rest", own_rest, u_rest.at[w], rest_send, rest_recv)
        if c >= 0:
            stage(it, c, s)
            if s == 0 and c == chunks - 1:
                row_exchange(it)
        else:
            step = left_update(it + 1) if it + 1 < ITERS else row_step(it)
            step_sum = step if step_sum is None else step_sum + step
            if it + 1 == ITERS:
                step_exchange(step_sum)
    finish("step")
    out = u_in[...]
    for j in range(wide):
        out = out + steps[j].astype(F32)
    u_out[...] = out
    for copy in pending:
        copy.wait_send()
    for copy in stores:
        copy.wait()


PARTS = 4


def flush(a, b, c, a_out, b_out, c_out, sem):
    copies = [pltpu.make_async_copy(b, b_out, sem.at[2 * PARTS])]
    rows = c.shape[0] // PARTS
    cols = a.shape[2] // PARTS
    for i in range(PARTS):
        at = pl.ds(i * rows, rows)
        copies.append(pltpu.make_async_copy(c.at[at], c_out.at[at], sem.at[i]))
        at = pl.ds(i * cols, cols)
        copies.append(
            pltpu.make_async_copy(a.at[:, :, at], a_out.at[:, :, at], sem.at[PARTS + i])
        )
    for copy in copies:
        copy.start()
    for copy in copies:
        copy.wait()


def local(
    pieces, destination, first_offset, valid_length, midpoint_factor, offset_factor, threshold
):
    wide = lax.axis_size("wide")
    rows, rank2 = midpoint_factor.shape
    cols = offset_factor.shape[0]
    chunk = max(cols // CHUNKS, 16 * wide)
    chunks = cols // chunk
    bits = wide.bit_length() - 1
    vmem = pl.BlockSpec(memory_space=pltpu.VMEM)
    hbm = pl.BlockSpec(memory_space=pltpu.HBM)
    dma = pltpu.SemaphoreType.DMA
    results = pl.pallas_call(
        functools.partial(kernel, wide, chunk),
        out_shape=(
            jax.ShapeDtypeStruct(pieces.shape, BF16),
            jax.ShapeDtypeStruct(midpoint_factor.shape, F32),
            jax.ShapeDtypeStruct(offset_factor.shape, F32),
        ),
        in_specs=[hbm] * 7,
        out_specs=(hbm, vmem, hbm),
        scratch_shapes=[
            pltpu.VMEM(pieces.shape, BF16),
            pltpu.VMEM((1, rows), jnp.int32),
            pltpu.VMEM((1, rows), jnp.int32),
            pltpu.VMEM((1, rows), jnp.int32),
            pltpu.VMEM((rows, rank2), F32),
            pltpu.VMEM((cols, rank2), F32),
            pltpu.VMEM((1, cols), F32),
            dma((7,)),
            dma((2, chunks)),
            pltpu.VMEM((cols, rank2), BF16),
            pltpu.VMEM((cols, rank2), F32),
            pltpu.VMEM((ITERS, cols, rank2), BF16),
            pltpu.VMEM((ITERS, chunks, chunk, rank2), BF16),
            pltpu.VMEM((ITERS, cols, rank2), BF16),
            pltpu.VMEM((2 * rows, rank2), BF16),
            pltpu.VMEM((rows, rank2), F32),
            pltpu.VMEM((2 * rows, rank2), F32),
            pltpu.VMEM((wide, rows, rank2), BF16),
            pltpu.VMEM((wide, rows, rank2), BF16),
            pltpu.VMEM((rows, rank2), BF16),
            pltpu.VMEM((rows, rank2), BF16),
            pltpu.VMEM((ITERS, 8, rank2), F32),
            pltpu.VMEM((ITERS, wide, 8, rank2), F32),
            pltpu.VMEM((ITERS, rows + 8, rank2), F32),
            pltpu.VMEM((ITERS, rows + 8, rank2), F32),
            pltpu.VMEM((wide, rows, rank2), BF16),
            pltpu.VMEM((wide, rows, rank2), BF16),
            dma((ITERS, chunks, bits)),
            dma((ITERS, chunks, bits)),
            dma((ITERS, chunks, bits)),
            dma((ITERS, chunks, bits)),
            dma((wide - 1,)),
            dma((wide - 1,)),
            dma((wide - 1,)),
            dma((wide - 1,)),
            dma((ITERS, wide - 1)),
            dma((ITERS, wide - 1)),
            dma((ITERS,)),
            dma((ITERS,)),
            dma((wide - 1,)),
            dma((wide - 1,)),
        ],
        compiler_params=pltpu.CompilerParams(
            collective_id=0, has_side_effects=True, vmem_limit_bytes=56 * 1024 * 1024
        ),
        cost_estimate=pl.CostEstimate(
            flops=ITERS * 3 * 4 * rows * rank2 * cols,
            bytes_accessed=12 * cols * rank2,
            transcendentals=0,
        ),
    )(
        pieces,
        destination.reshape(1, rows),
        first_offset.reshape(1, rows),
        valid_length.reshape(1, rows),
        midpoint_factor,
        offset_factor,
        threshold.reshape(1, cols),
    )
    return pl.pallas_call(
        flush,
        out_shape=tuple(jax.ShapeDtypeStruct(r.shape, r.dtype) for r in results),
        in_specs=[hbm] * 3,
        out_specs=(hbm,) * 3,
        scratch_shapes=[dma((2 * PARTS + 1,))],
        compiler_params=pltpu.CompilerParams(vmem_limit_bytes=56 * 1024 * 1024),
    )(*results)


def solution(mesh):
    placed = (
        P(None, ("groups", "wide"), "narrow"),
        P("wide"),
        P("wide"),
        P("wide"),
        P(("groups", "wide"), None),
        P(("groups", "narrow"), None),
        P(("groups", "narrow")),
    )
    return jax.shard_map(
        local,
        mesh=mesh,
        in_specs=placed,
        out_specs=(
            P(None, ("groups", "wide"), "narrow"),
            P(("groups", "wide"), None),
            P(("groups", "narrow"), None),
        ),
        check_vma=False,
    )
```

```python
import functools

import jax
import jax.numpy as jnp
from jax import lax
from jax.experimental import pallas as pl
from jax.experimental.pallas import tpu as pltpu
from jax.sharding import PartitionSpec as P

ITERS = 2
CHUNKS = 8

epsilon = 1e-06
F32 = jnp.float32
BF16 = jnp.bfloat16
MESH = pl.DeviceIdType.MESH


def order_of(c, bits):
    base = list(range(bits))
    if c % 2 and bits > 1:
        base[0], base[1] = base[1], base[0]
    return base


def plan(chunks, chunk, bits):
    delay, rate, work, step = 1.6, 45e3, 0.6 + 0.8 * chunk / 512, 0.15
    last = 2 * bits
    now, busy, arrived, order = 0.0, [0.0] * bits, {}, []
    stage_at = {(it, c): 0 for it in range(ITERS) for c in range(chunks)}
    computed, row_sent, row_done = [0] * ITERS, [None] * ITERS, [False] * ITERS
    while True:
        ready = []
        for (it, c), s in stage_at.items():
            if s == 0:
                allowed = it == 0 or (row_done[it - 1] and stage_at[it - 1, c] > last)
                if c == computed[it] and allowed:
                    ready.append((now, it, c, s))
            elif s <= last:
                ready.append((arrived[it, c], it, c, s))
        for it in range(ITERS):
            if row_sent[it] is not None and not row_done[it]:
                ready.append((row_sent[it] + delay, it, -1, 0))
        if not ready:
            return order
        when, it, c, s = min(ready)
        now = max(now, when)
        order.append((it, c, s))
        if c < 0:
            row_done[it] = True
            now += 0.5
            continue
        now += work if s == 0 else step + 0.2 * chunk / 512
        if s == 0:
            computed[it] += 1
            if computed[it] == chunks:
                row_sent[it] = now
        if s < last:
            r = s if s < bits else last - 1 - s
            b = order_of(c, bits)[r]
            start = max(busy[b], now)
            busy[b] = start + (chunk * 256 >> (r + 1)) / (rate if b < 2 else rate / 2)
            arrived[it, c] = busy[b] + delay
        stage_at[it, c] += 1


def swap_halves(x):
    half = x.shape[1] // 2
    return jnp.concatenate([x[:, half:], x[:, :half]], 1)


def turned(x):
    half = x.shape[1] // 2
    return jnp.concatenate([x[:, half:], -x[:, :half]], 1)


def kernel(
    wide,
    chunk,
    pieces_hbm,
    dest_hbm,
    first_hbm,
    valid_hbm,
    u_hbm,
    v_hbm,
    thr_hbm,
    sp_hbm,
    u_out,
    v_out_hbm,
    pieces,
    dest,
    first,
    valid,
    u_in,
    v_now,
    thr,
    in_sem,
    out_sem,
    v_low,
    acc,
    sent,
    got,
    total,
    stack,
    u_seg,
    row_acc,
    u_high,
    u_rest,
    own_high,
    own_rest,
    norm_own,
    norms,
    row_own,
    row_peer,
    step_own,
    steps,
    rs_send,
    rs_recv,
    ag_send,
    ag_recv,
    high_send,
    high_recv,
    rest_send,
    rest_recv,
    norm_send,
    norm_recv,
    row_send,
    row_recv,
    step_send,
    step_recv,
):
    g = lax.axis_index("groups")
    w = lax.axis_index("wide")
    n = lax.axis_index("narrow")
    rows, rank2 = u_in.shape
    cols = v_now.shape[0]
    chunks = cols // chunk
    bits = wide.bit_length() - 1
    peers = [lax.bitwise_xor(w, jnp.int32(j)) for j in range(1, wide)]
    side = 1 - n
    pending = []
    loads = [
        pltpu.make_async_copy(src, dst, in_sem.at[i])
        for i, (src, dst) in enumerate(
            [
                (u_hbm, u_in),
                (dest_hbm, dest),
                (first_hbm, first),
                (valid_hbm, valid),
                (v_hbm, v_now),
                (thr_hbm, thr),
                (pieces_hbm, pieces),
            ]
        )
    ]
    for load in loads:
        load.start()
    stores = []

    def store(src, dst, sem):
        copy = pltpu.make_async_copy(src, dst, sem)
        copy.start()
        stores.append(copy)

    def send(src, dst, s_sem, r_sem, to_wide=None, to_narrow=None):
        copy = pltpu.make_async_remote_copy(
            src_ref=src,
            dst_ref=dst,
            send_sem=s_sem,
            recv_sem=r_sem,
            device_id=(g, w if to_wide is None else to_wide, n if to_narrow is None else to_narrow),
            device_id_type=MESH,
        )
        copy.start()
        pending.append(copy)
        return copy

    barrier = pltpu.get_barrier_semaphore()
    for p in peers:
        pl.semaphore_signal(barrier, inc=1, device_id=(g, p, n), device_id_type=MESH)
    pl.semaphore_signal(barrier, inc=1, device_id=(g, w, side), device_id_type=MESH)

    loads[0].wait()
    u0 = u_in[...]
    high = u0.astype(BF16)
    own_high[...] = high
    own_rest[...] = (u0 - high.astype(F32)).astype(BF16)
    u_high[w] = own_high[...]
    u_rest[w] = own_rest[...]
    part = jnp.broadcast_to(jnp.sum(u0 * u0, 0, keepdims=True), (8, rank2))
    norm_own[0] = part
    norms[0, w] = part
    pl.semaphore_wait(barrier, wide)

    waits = {}

    def gather(name, src, dst, s_sem, r_sem):
        for j, p in enumerate(peers):
            waits.setdefault(name, []).append(
                send(src, dst, s_sem.at[j], r_sem.at[j], to_wide=p)
            )

    def finish(name):
        for copy in waits[name]:
            copy.wait_recv()

    gather("high", own_high, u_high.at[w], high_send, high_recv)
    gather("norm0", norm_own.at[0], norms.at[0, w], norm_send.at[0], norm_recv.at[0])

    for load in loads[1:5]:
        load.wait()
    eye = lax.broadcasted_iota(jnp.int32, (rows, rows), 0) == lax.broadcasted_iota(
        jnp.int32, (rows, rows), 1
    )

    def column(ref):
        wide_row = jnp.broadcast_to(ref[...].astype(F32), (rows, rows))
        return jnp.sum(jnp.where(eye, wide_row, 0.0), 1, keepdims=True).astype(jnp.int32)

    dest_col = column(dest)
    begin_col = column(first) - n * cols
    end_col = begin_col + column(valid)
    pick = (
        lax.broadcasted_iota(jnp.int32, (rows, wide * rows), 1) == dest_col
    ).astype(BF16)

    square = jnp.zeros((1, rank2), F32)
    for c in range(chunks):
        at = pl.ds(c * chunk, chunk)
        v = v_now[at]
        v_low[at] = v.astype(BF16)
        square = square + jnp.sum(v * v, 0, keepdims=True)
    squares = [square, jnp.zeros((1, rank2), F32)]

    def left_ready(value):
        low = value.astype(BF16)
        stack[:rows] = low
        stack[rows:] = turned(low.astype(F32)).astype(BF16)

    for load in loads[5:]:
        load.wait()
    finish("high")
    picked_high = jnp.dot(
        pick, u_high[...].reshape(wide * rows, rank2), preferred_element_type=F32
    )
    left_ready(picked_high)

    def left_scale(it):
        finish("norm%d" % it)
        s = norms[it, 0, :1]
        for j in range(1, wide):
            s = s + norms[it, j, :1]
        return 1.0 / (s + swap_halves(s) + epsilon)

    scale = [None] * ITERS
    flights = {}

    def bit_of(b):
        return lax.bitwise_and(lax.shift_right_logical(w, jnp.int32(b)), 1)

    def place(c, s):
        start, size = jnp.int32(c * chunk), chunk
        for b in order_of(c, bits)[:s]:
            size //= 2
            start = start + bit_of(b) * size
        return pl.multiple_of(start, size), size

    def scatter_send(it, c, s):
        b = order_of(c, bits)[s]
        start, size = place(c, s)
        half = size // 2
        away = pl.ds(pl.multiple_of(start + (1 - bit_of(b)) * half, half), half)
        sent[it, away] = acc[away].astype(BF16)
        slot = chunk - size
        flights[it, c, s] = send(
            sent.at[it, away],
            got.at[it, c, pl.ds(slot, half)],
            rs_send.at[it, c, s],
            rs_recv.at[it, c, s],
            to_wide=lax.bitwise_xor(w, jnp.int32(1 << b)),
        )

    def scatter_take(it, c, s):
        flights[it, c, s].wait_recv()
        start, size = place(c, s + 1)
        mine = pl.ds(start, size)
        summed = acc[mine] + got[it, c, pl.ds(chunk - 2 * size, size)].astype(F32)
        if s == bits - 1:
            total[it, mine] = summed.astype(BF16)
        else:
            acc[mine] = summed

    def gather_send(it, c, s):
        start, size = place(c, s + 1)
        mine = pl.ds(start, size)
        flights[it, c, "g", s] = send(
            total.at[it, mine],
            total.at[it, mine],
            ag_send.at[it, c, s],
            ag_recv.at[it, c, s],
            to_wide=lax.bitwise_xor(w, jnp.int32(1 << order_of(c, bits)[s])),
        )

    def compute(it, c):
        at = pl.ds(c * chunk, chunk)
        low = v_low[at]
        left = stack[...]
        model = lax.dot_general(left, low, (((1,), (1,)), ((), ())), preferred_element_type=F32)
        lane = lax.broadcasted_iota(jnp.int32, (rows, chunk), 1) + c * chunk
        inside = (lane >= begin_col) & (lane < end_col)
        real = jnp.where(inside, pieces[0, :, at].astype(F32) - model[:rows], 0.0)
        imag = jnp.where(inside, pieces[1, :, at].astype(F32) - model[rows:], 0.0)
        keep = jnp.minimum(thr[:, at] * lax.rsqrt(real * real + imag * imag), 1.0)
        err_real = real * keep
        err_imag = imag * keep
        if it == ITERS - 1:
            pieces[0, :, at] = (real - err_real).astype(BF16)
            pieces[1, :, at] = (imag - err_imag).astype(BF16)
            store(pieces.at[:, :, at], sp_hbm.at[:, :, at], out_sem.at[0, c])
        err = jnp.concatenate([err_real, err_imag], 0).astype(BF16)
        row = jnp.dot(err, low, preferred_element_type=F32)
        row_acc[...] = row if c == 0 else row_acc[...] + row
        acc[at] = lax.dot_general(err, left, (((0,), (0,)), ((), ())), preferred_element_type=F32)
        scatter_send(it, c, 0)

    def row_exchange(it):
        row = row_acc[...]
        row_own[it, :rows] = row[:rows] - turned(row[rows:])
        row_own[it, rows:] = jnp.broadcast_to(squares[it], (8, rank2))
        flights[it, "row"] = send(
            row_own.at[it], row_peer.at[it], row_send.at[it], row_recv.at[it], to_narrow=side
        )

    def row_step(it):
        flights[it, "row"].wait_recv()
        both = row_own[it] + row_peer[it]
        square = both[rows : rows + 1]
        return both[:rows] / (square + swap_halves(square) + epsilon)

    def update(it, c):
        at = pl.ds(c * chunk, chunk)
        if scale[it] is None:
            scale[it] = left_scale(it)
        new = v_now[at] + total[it, at].astype(F32) * scale[it]
        v_now[at] = new
        if it < ITERS - 1:
            v_low[at] = new.astype(BF16)
            squares[it + 1] = squares[it + 1] + jnp.sum(new * new, 0, keepdims=True)
        else:
            store(v_now.at[at], v_out_hbm.at[at], out_sem.at[1, c])

    def stage(it, c, s):
        if s == 0:
            compute(it, c)
        elif s <= bits:
            scatter_take(it, c, s - 1)
            if s < bits:
                scatter_send(it, c, s)
            else:
                gather_send(it, c, bits - 1)
        else:
            r = 2 * bits - s
            flights[it, c, "g", r].wait_recv()
            if r > 0:
                gather_send(it, c, r - 1)
            else:
                update(it, c)

    def left_update(it):
        step = row_step(it - 1)
        if it == 1:
            finish("rest")
            u_seg[...] = picked_high + jnp.dot(
                pick, u_rest[...].reshape(wide * rows, rank2), preferred_element_type=F32
            )
        value = u_seg[...] + step
        u_seg[...] = value
        left_ready(value)
        part = jnp.broadcast_to(jnp.sum(value * value, 0, keepdims=True), (8, rank2))
        norm_own[it] = part
        norms[it, w] = part
        gather(
            "norm%d" % it, norm_own.at[it], norms.at[it, w], norm_send.at[it], norm_recv.at[it]
        )
        return step

    def step_exchange(step_sum):
        spread = (
            lax.broadcasted_iota(jnp.int32, (wide * rows, rows), 0)
            == jnp.broadcast_to(dest[...], (wide * rows, rows))
        ).astype(BF16)
        placed = jnp.dot(spread, step_sum.astype(BF16), preferred_element_type=F32)
        step_own[...] = placed.astype(BF16).reshape(wide, rows, rank2)
        steps[w] = step_own[w]
        for j, p in enumerate(peers):
            waits.setdefault("step", []).append(
                send(step_own.at[p], steps.at[w], step_send.at[j], step_recv.at[j], to_wide=p)
            )

    last = 2 * bits
    step_sum = None
    for index, (it, c, s) in enumerate(plan(chunks, chunk, bits)):
        if index == min(2, chunks - 1):
            gather("rest", own_rest, u_rest.at[w], rest_send, rest_recv)
        if c >= 0:
            stage(it, c, s)
            if s == 0 and c == chunks - 1:
                row_exchange(it)
        else:
            step = left_update(it + 1) if it + 1 < ITERS else row_step(it)
            step_sum = step if step_sum is None else step_sum + step
            if it + 1 == ITERS:
                step_exchange(step_sum)
    finish("step")
    out = u_in[...]
    for j in range(wide):
        out = out + steps[j].astype(F32)
    u_out[...] = out
    for copy in pending:
        copy.wait_send()
    for copy in stores:
        copy.wait()


PARTS = 4


def flush(a, b, c, a_out, b_out, c_out, a_held, b_held, c_held, in_sem, out_sem):
    rows = c.shape[0] // PARTS
    cols = a.shape[2] // PARTS
    moves = []
    for i in range(PARTS):
        at = pl.ds(i * rows, rows)
        moves.append((c.at[at], c_held.at[at], c_out.at[at]))
        at = pl.ds(i * cols, cols)
        moves.append((a.at[:, :, at], a_held.at[:, :, at], a_out.at[:, :, at]))
    moves.append((b, b_held, b_out))
    loads = [
        pltpu.make_async_copy(src, held, in_sem.at[i]) for i, (src, held, _) in enumerate(moves)
    ]
    stores = [
        pltpu.make_async_copy(held, dst, out_sem.at[i]) for i, (_, held, dst) in enumerate(moves)
    ]
    for load in loads:
        load.start()
    for load, store in zip(loads, stores):
        load.wait()
        store.start()
    for store in stores:
        store.wait()


def local(
    pieces, destination, first_offset, valid_length, midpoint_factor, offset_factor, threshold
):
    wide = lax.axis_size("wide")
    rows, rank2 = midpoint_factor.shape
    cols = offset_factor.shape[0]
    chunk = max(cols // CHUNKS, 16 * wide)
    chunks = cols // chunk
    bits = wide.bit_length() - 1
    vmem = pl.BlockSpec(memory_space=pltpu.VMEM)
    hbm = pl.BlockSpec(memory_space=pltpu.HBM)
    dma = pltpu.SemaphoreType.DMA
    results = pl.pallas_call(
        functools.partial(kernel, wide, chunk),
        out_shape=(
            jax.ShapeDtypeStruct(pieces.shape, BF16),
            jax.ShapeDtypeStruct(midpoint_factor.shape, F32),
            jax.ShapeDtypeStruct(offset_factor.shape, F32),
        ),
        in_specs=[hbm] * 7,
        out_specs=(hbm, vmem, hbm),
        scratch_shapes=[
            pltpu.VMEM(pieces.shape, BF16),
            pltpu.VMEM((1, rows), jnp.int32),
            pltpu.VMEM((1, rows), jnp.int32),
            pltpu.VMEM((1, rows), jnp.int32),
            pltpu.VMEM((rows, rank2), F32),
            pltpu.VMEM((cols, rank2), F32),
            pltpu.VMEM((1, cols), F32),
            dma((7,)),
            dma((2, chunks)),
            pltpu.VMEM((cols, rank2), BF16),
            pltpu.VMEM((cols, rank2), F32),
            pltpu.VMEM((ITERS, cols, rank2), BF16),
            pltpu.VMEM((ITERS, chunks, chunk, rank2), BF16),
            pltpu.VMEM((ITERS, cols, rank2), BF16),
            pltpu.VMEM((2 * rows, rank2), BF16),
            pltpu.VMEM((rows, rank2), F32),
            pltpu.VMEM((2 * rows, rank2), F32),
            pltpu.VMEM((wide, rows, rank2), BF16),
            pltpu.VMEM((wide, rows, rank2), BF16),
            pltpu.VMEM((rows, rank2), BF16),
            pltpu.VMEM((rows, rank2), BF16),
            pltpu.VMEM((ITERS, 8, rank2), F32),
            pltpu.VMEM((ITERS, wide, 8, rank2), F32),
            pltpu.VMEM((ITERS, rows + 8, rank2), F32),
            pltpu.VMEM((ITERS, rows + 8, rank2), F32),
            pltpu.VMEM((wide, rows, rank2), BF16),
            pltpu.VMEM((wide, rows, rank2), BF16),
            dma((ITERS, chunks, bits)),
            dma((ITERS, chunks, bits)),
            dma((ITERS, chunks, bits)),
            dma((ITERS, chunks, bits)),
            dma((wide - 1,)),
            dma((wide - 1,)),
            dma((wide - 1,)),
            dma((wide - 1,)),
            dma((ITERS, wide - 1)),
            dma((ITERS, wide - 1)),
            dma((ITERS,)),
            dma((ITERS,)),
            dma((wide - 1,)),
            dma((wide - 1,)),
        ],
        compiler_params=pltpu.CompilerParams(
            collective_id=0, has_side_effects=True, vmem_limit_bytes=56 * 1024 * 1024
        ),
        cost_estimate=pl.CostEstimate(
            flops=ITERS * 3 * 4 * rows * rank2 * cols,
            bytes_accessed=12 * cols * rank2,
            transcendentals=0,
        ),
    )(
        pieces,
        destination.reshape(1, rows),
        first_offset.reshape(1, rows),
        valid_length.reshape(1, rows),
        midpoint_factor,
        offset_factor,
        threshold.reshape(1, cols),
    )
    return pl.pallas_call(
        flush,
        out_shape=tuple(jax.ShapeDtypeStruct(r.shape, r.dtype) for r in results),
        in_specs=[hbm] * 3,
        out_specs=(hbm,) * 3,
        scratch_shapes=[pltpu.VMEM(r.shape, r.dtype) for r in results]
        + [dma((2 * PARTS + 1,)), dma((2 * PARTS + 1,))],
        compiler_params=pltpu.CompilerParams(vmem_limit_bytes=56 * 1024 * 1024),
    )(*results)


def solution(mesh):
    placed = (
        P(None, ("groups", "wide"), "narrow"),
        P("wide"),
        P("wide"),
        P("wide"),
        P(("groups", "wide"), None),
        P(("groups", "narrow"), None),
        P(("groups", "narrow")),
    )
    return jax.shard_map(
        local,
        mesh=mesh,
        in_specs=placed,
        out_specs=(
            P(None, ("groups", "wide"), "narrow"),
            P(("groups", "wide"), None),
            P(("groups", "narrow"), None),
        ),
        check_vma=False,
    )
```

```python
import functools

import jax
import jax.numpy as jnp
from jax import lax
from jax.experimental import pallas as pl
from jax.experimental.pallas import tpu as pltpu
from jax.sharding import PartitionSpec as P

ITERS = 2
CHUNKS = 8

epsilon = 1e-06
F32 = jnp.float32
BF16 = jnp.bfloat16
MESH = pl.DeviceIdType.MESH


def order_of(c, bits):
    base = list(range(bits))
    if c % 2 and bits > 1:
        base[0], base[1] = base[1], base[0]
    return base


def plan(chunks, bits):
    last = 2 * bits
    lag = [0]
    for s in range(last):
        lag.append(lag[-1] + max(2, 4 - min(s, last - 1 - s)))
    spacing = max(chunks, lag[last])
    events = []
    for it in range(ITERS):
        for c in range(chunks):
            for s in range(last + 1):
                events.append((it * spacing + c + lag[s], it, -s, c))
        events.append((min(it * spacing + chunks + 2, (it + 1) * spacing), it, 1, -1))
    return [(it, c, -s) for _, it, s, c in sorted(events)]


def swap_halves(x):
    half = x.shape[1] // 2
    return jnp.concatenate([x[:, half:], x[:, :half]], 1)


def turned(x):
    half = x.shape[1] // 2
    return jnp.concatenate([x[:, half:], -x[:, :half]], 1)


def kernel(
    wide,
    chunk,
    pieces_hbm,
    dest_hbm,
    first_hbm,
    valid_hbm,
    u_hbm,
    v_hbm,
    thr_hbm,
    sp_hbm,
    u_out,
    v_out_hbm,
    pieces,
    dest,
    first,
    valid,
    u_in,
    v_now,
    thr,
    in_sem,
    out_sem,
    v_low,
    acc,
    sent,
    got,
    total,
    stack,
    u_seg,
    row_acc,
    u_high,
    u_rest,
    own_high,
    own_rest,
    norm_own,
    norms,
    row_own,
    row_peer,
    step_own,
    steps,
    rs_send,
    rs_recv,
    ag_send,
    ag_recv,
    high_send,
    high_recv,
    rest_send,
    rest_recv,
    norm_send,
    norm_recv,
    row_send,
    row_recv,
    step_send,
    step_recv,
):
    g = lax.axis_index("groups")
    w = lax.axis_index("wide")
    n = lax.axis_index("narrow")
    rows, rank2 = u_in.shape
    cols = v_now.shape[0]
    chunks = cols // chunk
    bits = wide.bit_length() - 1
    peers = [lax.bitwise_xor(w, jnp.int32(j)) for j in range(1, wide)]
    side = 1 - n
    pending = []
    loads = [
        pltpu.make_async_copy(src, dst, in_sem.at[i])
        for i, (src, dst) in enumerate(
            [
                (u_hbm, u_in),
                (dest_hbm, dest),
                (first_hbm, first),
                (valid_hbm, valid),
                (v_hbm, v_now),
                (thr_hbm, thr),
                (pieces_hbm, pieces),
            ]
        )
    ]
    for load in loads:
        load.start()
    stores = []

    def store(src, dst, sem):
        copy = pltpu.make_async_copy(src, dst, sem)
        copy.start()
        stores.append(copy)

    def send(src, dst, s_sem, r_sem, to_wide=None, to_narrow=None):
        copy = pltpu.make_async_remote_copy(
            src_ref=src,
            dst_ref=dst,
            send_sem=s_sem,
            recv_sem=r_sem,
            device_id=(g, w if to_wide is None else to_wide, n if to_narrow is None else to_narrow),
            device_id_type=MESH,
        )
        copy.start()
        pending.append(copy)
        return copy

    barrier = pltpu.get_barrier_semaphore()
    for p in peers:
        pl.semaphore_signal(barrier, inc=1, device_id=(g, p, n), device_id_type=MESH)
    pl.semaphore_signal(barrier, inc=1, device_id=(g, w, side), device_id_type=MESH)

    loads[0].wait()
    u0 = u_in[...]
    high = u0.astype(BF16)
    own_high[...] = high
    own_rest[...] = (u0 - high.astype(F32)).astype(BF16)
    u_high[w] = own_high[...]
    u_rest[w] = own_rest[...]
    part = jnp.broadcast_to(jnp.sum(u0 * u0, 0, keepdims=True), (8, rank2))
    norm_own[0] = part
    norms[0, w] = part
    pl.semaphore_wait(barrier, wide)

    waits = {}

    def gather(name, src, dst, s_sem, r_sem):
        for j, p in enumerate(peers):
            waits.setdefault(name, []).append(
                send(src, dst, s_sem.at[j], r_sem.at[j], to_wide=p)
            )

    def finish(name):
        for copy in waits[name]:
            copy.wait_recv()

    gather("high", own_high, u_high.at[w], high_send, high_recv)
    gather("norm0", norm_own.at[0], norms.at[0, w], norm_send.at[0], norm_recv.at[0])

    for load in loads[1:5]:
        load.wait()
    eye = lax.broadcasted_iota(jnp.int32, (rows, rows), 0) == lax.broadcasted_iota(
        jnp.int32, (rows, rows), 1
    )

    def column(ref):
        wide_row = jnp.broadcast_to(ref[...].astype(F32), (rows, rows))
        return jnp.sum(jnp.where(eye, wide_row, 0.0), 1, keepdims=True).astype(jnp.int32)

    dest_col = column(dest)
    begin_col = column(first) - n * cols
    end_col = begin_col + column(valid)
    pick = (
        lax.broadcasted_iota(jnp.int32, (rows, wide * rows), 1) == dest_col
    ).astype(BF16)

    square = jnp.zeros((1, rank2), F32)
    for c in range(chunks):
        at = pl.ds(c * chunk, chunk)
        v = v_now[at]
        v_low[at] = v.astype(BF16)
        square = square + jnp.sum(v * v, 0, keepdims=True)
    squares = [square, jnp.zeros((1, rank2), F32)]

    def left_ready(value):
        low = value.astype(BF16)
        stack[:rows] = low
        stack[rows:] = turned(low.astype(F32)).astype(BF16)

    for load in loads[5:]:
        load.wait()
    finish("high")
    picked_high = jnp.dot(
        pick, u_high[...].reshape(wide * rows, rank2), preferred_element_type=F32
    )
    left_ready(picked_high)

    def left_scale(it):
        finish("norm%d" % it)
        s = norms[it, 0, :1]
        for j in range(1, wide):
            s = s + norms[it, j, :1]
        return 1.0 / (s + swap_halves(s) + epsilon)

    scale = [None] * ITERS
    flights = {}

    def bit_of(b):
        return lax.bitwise_and(lax.shift_right_logical(w, jnp.int32(b)), 1)

    def place(c, s):
        start, size = jnp.int32(c * chunk), chunk
        for b in order_of(c, bits)[:s]:
            size //= 2
            start = start + bit_of(b) * size
        return pl.multiple_of(start, size), size

    def scatter_send(it, c, s):
        b = order_of(c, bits)[s]
        start, size = place(c, s)
        half = size // 2
        away = pl.ds(pl.multiple_of(start + (1 - bit_of(b)) * half, half), half)
        sent[it, away] = acc[away].astype(BF16)
        slot = chunk - size
        flights[it, c, s] = send(
            sent.at[it, away],
            got.at[it, c, pl.ds(slot, half)],
            rs_send.at[it, c, s],
            rs_recv.at[it, c, s],
            to_wide=lax.bitwise_xor(w, jnp.int32(1 << b)),
        )

    def scatter_take(it, c, s):
        flights[it, c, s].wait_recv()
        start, size = place(c, s + 1)
        mine = pl.ds(start, size)
        summed = acc[mine] + got[it, c, pl.ds(chunk - 2 * size, size)].astype(F32)
        if s == bits - 1:
            total[it, mine] = summed.astype(BF16)
        else:
            acc[mine] = summed

    def gather_send(it, c, s):
        start, size = place(c, s + 1)
        mine = pl.ds(start, size)
        flights[it, c, "g", s] = send(
            total.at[it, mine],
            total.at[it, mine],
            ag_send.at[it, c, s],
            ag_recv.at[it, c, s],
            to_wide=lax.bitwise_xor(w, jnp.int32(1 << order_of(c, bits)[s])),
        )

    def compute(it, c):
        at = pl.ds(c * chunk, chunk)
        low = v_low[at]
        left = stack[...]
        model = lax.dot_general(left, low, (((1,), (1,)), ((), ())), preferred_element_type=F32)
        lane = lax.broadcasted_iota(jnp.int32, (rows, chunk), 1) + c * chunk
        inside = (lane >= begin_col) & (lane < end_col)
        real = jnp.where(inside, pieces[0, :, at].astype(F32) - model[:rows], 0.0)
        imag = jnp.where(inside, pieces[1, :, at].astype(F32) - model[rows:], 0.0)
        keep = jnp.minimum(thr[:, at] * lax.rsqrt(real * real + imag * imag), 1.0)
        err_real = real * keep
        err_imag = imag * keep
        if it == ITERS - 1:
            pieces[0, :, at] = (real - err_real).astype(BF16)
            pieces[1, :, at] = (imag - err_imag).astype(BF16)
            store(pieces.at[:, :, at], sp_hbm.at[:, :, at], out_sem.at[0, c])
        err = jnp.concatenate([err_real, err_imag], 0).astype(BF16)
        row = jnp.dot(err, low, preferred_element_type=F32)
        row_acc[...] = row if c == 0 else row_acc[...] + row
        acc[at] = lax.dot_general(err, left, (((0,), (0,)), ((), ())), preferred_element_type=F32)
        scatter_send(it, c, 0)

    def row_exchange(it):
        row = row_acc[...]
        row_own[it, :rows] = row[:rows] - turned(row[rows:])
        row_own[it, rows:] = jnp.broadcast_to(squares[it], (8, rank2))
        flights[it, "row"] = send(
            row_own.at[it], row_peer.at[it], row_send.at[it], row_recv.at[it], to_narrow=side
        )

    def row_step(it):
        flights[it, "row"].wait_recv()
        both = row_own[it] + row_peer[it]
        square = both[rows : rows + 1]
        return both[:rows] / (square + swap_halves(square) + epsilon)

    def update(it, c):
        at = pl.ds(c * chunk, chunk)
        if scale[it] is None:
            scale[it] = left_scale(it)
        new = v_now[at] + total[it, at].astype(F32) * scale[it]
        v_now[at] = new
        if it < ITERS - 1:
            v_low[at] = new.astype(BF16)
            squares[it + 1] = squares[it + 1] + jnp.sum(new * new, 0, keepdims=True)
        else:
            store(v_now.at[at], v_out_hbm.at[at], out_sem.at[1, c])

    def stage(it, c, s):
        if s == 0:
            compute(it, c)
        elif s <= bits:
            scatter_take(it, c, s - 1)
            if s < bits:
                scatter_send(it, c, s)
            else:
                gather_send(it, c, bits - 1)
        else:
            r = 2 * bits - s
            flights[it, c, "g", r].wait_recv()
            if r > 0:
                gather_send(it, c, r - 1)
            else:
                update(it, c)

    def left_update(it):
        step = row_step(it - 1)
        if it == 1:
            finish("rest")
            u_seg[...] = picked_high + jnp.dot(
                pick, u_rest[...].reshape(wide * rows, rank2), preferred_element_type=F32
            )
        value = u_seg[...] + step
        u_seg[...] = value
        left_ready(value)
        part = jnp.broadcast_to(jnp.sum(value * value, 0, keepdims=True), (8, rank2))
        norm_own[it] = part
        norms[it, w] = part
        gather(
            "norm%d" % it, norm_own.at[it], norms.at[it, w], norm_send.at[it], norm_recv.at[it]
        )
        return step

    def step_exchange(step_sum):
        spread = (
            lax.broadcasted_iota(jnp.int32, (wide * rows, rows), 0)
            == jnp.broadcast_to(dest[...], (wide * rows, rows))
        ).astype(BF16)
        placed = jnp.dot(spread, step_sum.astype(BF16), preferred_element_type=F32)
        step_own[...] = placed.astype(BF16).reshape(wide, rows, rank2)
        steps[w] = step_own[w]
        for j, p in enumerate(peers):
            waits.setdefault("step", []).append(
                send(step_own.at[p], steps.at[w], step_send.at[j], step_recv.at[j], to_wide=p)
            )

    last = 2 * bits
    step_sum = None
    for index, (it, c, s) in enumerate(plan(chunks, bits)):
        if index == min(2, chunks - 1):
            gather("rest", own_rest, u_rest.at[w], rest_send, rest_recv)
        if c >= 0:
            stage(it, c, s)
            if s == 0 and c == chunks - 1:
                row_exchange(it)
        else:
            step = left_update(it + 1) if it + 1 < ITERS else row_step(it)
            step_sum = step if step_sum is None else step_sum + step
            if it + 1 == ITERS:
                step_exchange(step_sum)
    finish("step")
    out = u_in[...]
    for j in range(wide):
        out = out + steps[j].astype(F32)
    u_out[...] = out
    for copy in pending:
        copy.wait_send()
    for copy in stores:
        copy.wait()


PARTS = 4


def flush(a, b, c, a_out, b_out, c_out, a_held, b_held, c_held, in_sem, out_sem):
    rows = c.shape[0] // PARTS
    cols = a.shape[2] // PARTS
    moves = []
    for i in range(PARTS):
        at = pl.ds(i * rows, rows)
        moves.append((c.at[at], c_held.at[at], c_out.at[at]))
        at = pl.ds(i * cols, cols)
        moves.append((a.at[:, :, at], a_held.at[:, :, at], a_out.at[:, :, at]))
    moves.append((b, b_held, b_out))
    loads = [
        pltpu.make_async_copy(src, held, in_sem.at[i]) for i, (src, held, _) in enumerate(moves)
    ]
    stores = [
        pltpu.make_async_copy(held, dst, out_sem.at[i]) for i, (_, held, dst) in enumerate(moves)
    ]
    for load in loads:
        load.start()
    for load, store in zip(loads, stores):
        load.wait()
        store.start()
    for store in stores:
        store.wait()


def local(
    pieces, destination, first_offset, valid_length, midpoint_factor, offset_factor, threshold
):
    wide = lax.axis_size("wide")
    rows, rank2 = midpoint_factor.shape
    cols = offset_factor.shape[0]
    chunk = max(cols // CHUNKS, 16 * wide)
    chunks = cols // chunk
    bits = wide.bit_length() - 1
    vmem = pl.BlockSpec(memory_space=pltpu.VMEM)
    hbm = pl.BlockSpec(memory_space=pltpu.HBM)
    dma = pltpu.SemaphoreType.DMA
    results = pl.pallas_call(
        functools.partial(kernel, wide, chunk),
        out_shape=(
            jax.ShapeDtypeStruct(pieces.shape, BF16),
            jax.ShapeDtypeStruct(midpoint_factor.shape, F32),
            jax.ShapeDtypeStruct(offset_factor.shape, F32),
        ),
        in_specs=[hbm] * 7,
        out_specs=(hbm, vmem, hbm),
        scratch_shapes=[
            pltpu.VMEM(pieces.shape, BF16),
            pltpu.VMEM((1, rows), jnp.int32),
            pltpu.VMEM((1, rows), jnp.int32),
            pltpu.VMEM((1, rows), jnp.int32),
            pltpu.VMEM((rows, rank2), F32),
            pltpu.VMEM((cols, rank2), F32),
            pltpu.VMEM((1, cols), F32),
            dma((7,)),
            dma((2, chunks)),
            pltpu.VMEM((cols, rank2), BF16),
            pltpu.VMEM((cols, rank2), F32),
            pltpu.VMEM((ITERS, cols, rank2), BF16),
            pltpu.VMEM((ITERS, chunks, chunk, rank2), BF16),
            pltpu.VMEM((ITERS, cols, rank2), BF16),
            pltpu.VMEM((2 * rows, rank2), BF16),
            pltpu.VMEM((rows, rank2), F32),
            pltpu.VMEM((2 * rows, rank2), F32),
            pltpu.VMEM((wide, rows, rank2), BF16),
            pltpu.VMEM((wide, rows, rank2), BF16),
            pltpu.VMEM((rows, rank2), BF16),
            pltpu.VMEM((rows, rank2), BF16),
            pltpu.VMEM((ITERS, 8, rank2), F32),
            pltpu.VMEM((ITERS, wide, 8, rank2), F32),
            pltpu.VMEM((ITERS, rows + 8, rank2), F32),
            pltpu.VMEM((ITERS, rows + 8, rank2), F32),
            pltpu.VMEM((wide, rows, rank2), BF16),
            pltpu.VMEM((wide, rows, rank2), BF16),
            dma((ITERS, chunks, bits)),
            dma((ITERS, chunks, bits)),
            dma((ITERS, chunks, bits)),
            dma((ITERS, chunks, bits)),
            dma((wide - 1,)),
            dma((wide - 1,)),
            dma((wide - 1,)),
            dma((wide - 1,)),
            dma((ITERS, wide - 1)),
            dma((ITERS, wide - 1)),
            dma((ITERS,)),
            dma((ITERS,)),
            dma((wide - 1,)),
            dma((wide - 1,)),
        ],
        compiler_params=pltpu.CompilerParams(
            collective_id=0, has_side_effects=True, vmem_limit_bytes=56 * 1024 * 1024
        ),
        cost_estimate=pl.CostEstimate(
            flops=ITERS * 3 * 4 * rows * rank2 * cols,
            bytes_accessed=12 * cols * rank2,
            transcendentals=0,
        ),
    )(
        pieces,
        destination.reshape(1, rows),
        first_offset.reshape(1, rows),
        valid_length.reshape(1, rows),
        midpoint_factor,
        offset_factor,
        threshold.reshape(1, cols),
    )
    return pl.pallas_call(
        flush,
        out_shape=tuple(jax.ShapeDtypeStruct(r.shape, r.dtype) for r in results),
        in_specs=[hbm] * 3,
        out_specs=(hbm,) * 3,
        scratch_shapes=[pltpu.VMEM(r.shape, r.dtype) for r in results]
        + [dma((2 * PARTS + 1,)), dma((2 * PARTS + 1,))],
        compiler_params=pltpu.CompilerParams(vmem_limit_bytes=56 * 1024 * 1024),
    )(*results)


def solution(mesh):
    placed = (
        P(None, ("groups", "wide"), "narrow"),
        P("wide"),
        P("wide"),
        P("wide"),
        P(("groups", "wide"), None),
        P(("groups", "narrow"), None),
        P(("groups", "narrow")),
    )
    return jax.shard_map(
        local,
        mesh=mesh,
        in_specs=placed,
        out_specs=(
            P(None, ("groups", "wide"), "narrow"),
            P(("groups", "wide"), None),
            P(("groups", "narrow"), None),
        ),
        check_vma=False,
    )
```
